128 devices in a mesh: seq: 8 (over z_lo, x), batch: 4 (over y), shard: 4 (over z_hi, core).
Axes of the slice: x: 4, y: 4, z: 4 (z_hi: 2, z_lo: 2; z = z_hi * 2 + z_lo), core: 2. Of those that a mesh axis runs over, the one named last changes fastest.
Arguments:
- tokens: bfloat16 [16, 3072, 640], P(('batch', 'shard'), 'seq'), may hold values from -6 to 6
- cotangent: bfloat16 [16, 3072, 640], P(('batch', 'shard'), 'seq'), may hold values from -15 to 15
- positions: int32 [16, 3072], P(('batch', 'shard'), 'seq'), may hold values from 0 to 2688, as said below
- weight_qkv: float32 [640, 1536], P(('batch', 'shard')), may hold values from -0.25 to 0.25
- weight_out: float32 [1024, 640], P(('batch', 'shard')), may hold values from -0.1875 to 0.1875
- weight_up: float32 [640, 4096], P(('batch', 'shard')), may hold values from -0.25 to 0.25
- weight_down: float32 [2048, 640], P(('batch', 'shard')), may hold values from -0.125 to 0.125
- norm_gains: float32 [3072], P(('batch', 'shard')), may hold values from -0.15 to 0.15
- first_qkv: float32 [640, 1536], P(('batch', 'shard')), may hold values from -40 to 40
- first_out: float32 [1024, 640], P(('batch', 'shard')), may hold values from -128 to 128
- first_up: float32 [640, 4096], P(('batch', 'shard')), may hold values from -80 to 80
- first_down: float32 [2048, 640], P(('batch', 'shard')), may hold values from -128 to 128
- first_gains: float32 [3072], P(('batch', 'shard')), may hold values from -128 to 128
- second_qkv: float32 [640, 1536], P(('batch', 'shard')), may hold values from 232.98048 to 928.9728
- second_out: float32 [1024, 640], P(('batch', 'shard')), may hold values from 2585.3953 to 10321.92
- second_up: float32 [640, 4096], P(('batch', 'shard')), may hold values from 648.8064 to 2585.3953
- second_down: float32 [2048, 640], P(('batch', 'shard')), may hold values from 2585.3953 to 10321.92
- second_gains: float32 [3072], P(('batch', 'shard')), may hold values from 2585.3953 to 10321.92
Outputs:
- output_tokens: bfloat16 [16, 3072, 640], P(('batch', 'shard'), 'seq')
- grad_tokens: float32 [16, 3072, 640], P(('batch', 'shard'), 'seq')
- new_qkv: float32 [640, 1536], P(('batch', 'shard'))
- new_out: float32 [1024, 640], P(('batch', 'shard'))
- new_up: float32 [640, 4096], P(('batch', 'shard'))
- new_down: float32 [2048, 640], P(('batch', 'shard'))
- new_gains: float32 [3072], P(('batch', 'shard'))
- mean_qkv: float32 [640, 1536], P(('batch', 'shard'))
- mean_out: float32 [1024, 640], P(('batch', 'shard'))
- mean_up: float32 [640, 4096], P(('batch', 'shard'))
- mean_down: float32 [2048, 640], P(('batch', 'shard'))
- mean_gains: float32 [3072], P(('batch', 'shard'))
- square_qkv: float32 [640, 1536], P(('batch', 'shard'))
- square_out: float32 [1024, 640], P(('batch', 'shard'))
- square_up: float32 [640, 4096], P(('batch', 'shard'))
- square_down: float32 [2048, 640], P(('batch', 'shard'))
- square_gains: float32 [3072], P(('batch', 'shard'))
The draws below stay inside these ranges and needn't reach their ends.
Inputs may be any that keep to these rules, and one draw needn't show every extreme that they name: `positions`: each row of 3072 tokens holds three documents one after another (the first and last may be empty), and a token's position counts from its document's first token; the first and last documents together hold 383 tokens, so the middle one starts within the first 384 tokens, ends within the last 384, and has 2689 tokens.
All inputs are finite; a program needn't handle non-finite values.
Results may differ from the reference program's by a relative error of at most 0.018.
Values may be sent and summed in bfloat16 or wider, within the bound.
A program may use at most 128 MiB of HBM per device.

```python
import math
import jax
import jax.numpy as jnp
from jax import lax

D = 640
FF = 2048
HEADS = 4
HD = 256
WINDOW = 512
STEP = 10
LOCAL = 384
SEQ_LEN = 3072
GROUPS = 16
QKV = 1536
GAINS = 3072


def draw_positions(key, part):
    key = jax.random.fold_in(key, 7)
    head_len = jax.random.randint(key, (GROUPS, 1), 0, LOCAL)
    tail_len = LOCAL - 1 - head_len
    token_index = jnp.arange(SEQ_LEN, dtype=jnp.int32)[None, :]
    tail_start = SEQ_LEN - tail_len
    doc_start = jnp.where(token_index < head_len, 0, jnp.where(token_index < tail_start, head_len, tail_start))
    return (token_index - doc_start).astype(jnp.int32)


def draw_cotangent(key, part):
    key = jax.random.fold_in(key, 11)
    base = jnp.clip(jax.random.normal(key, (GROUPS, SEQ_LEN, D), jnp.float32), -6.0, 6.0)
    group_rank = jnp.arange(GROUPS, dtype=jnp.float32) / max(GROUPS - 1, 1)
    place_rank = jnp.arange(SEQ_LEN, dtype=jnp.float32) / max(SEQ_LEN - 1, 1)
    slope = 2.0
    spread = (1.0 + slope + slope * slope / 3.0) ** 0.5
    group_factor = (1.0 + slope * group_rank) / spread
    place_factor = (1.0 + slope * place_rank) / spread
    factor = group_factor[:, None, None] * place_factor[None, :, None]
    return (base * factor).astype(jnp.bfloat16)


def levels(stream_key, shape, split, low, high):
    def one(dim, blocks):
        heights = jax.random.uniform(jax.random.fold_in(jax.random.fold_in(stream_key, 6), dim), (blocks,), jnp.float32, low / len(split), high / len(split))
        return jnp.repeat(jnp.exp(heights), shape[dim] // blocks).reshape((-1,) + (1,) * (len(shape) - dim - 1))

    level = one(*split[0])
    for cut in split[1:]:
        level = level * one(*cut)
    return level


def scatter_about(stream_key, extent, scale, most, cuts=(), kind=jnp.bfloat16):
    level = levels(stream_key, extent, cuts, -0.22, 0.18) if cuts else 1.0
    values = jax.random.normal(stream_key, extent, jnp.float32) * scale * level
    return jnp.minimum(jnp.maximum(values, -most), most).astype(kind)


def setup_inputs(seed: int = 0) -> dict:
    splits = jax.random.split(jax.random.key(seed), 19)
    tokens = scatter_about(splits[0], (GROUPS, SEQ_LEN, D), 1.0, 6.0, ((0, 16), (1, 8)))
    cotangent = draw_cotangent(jax.random.fold_in(splits[18], 71), 0)
    positions = draw_positions(jax.random.fold_in(splits[18], 71), 0)
    weight_qkv = scatter_about(splits[3], (D, QKV), D ** -0.5, 0.25, ((0, 16),), jnp.float32)
    weight_out = scatter_about(splits[4], (HEADS * HD, D), (HEADS * HD) ** -0.5, 0.1875, ((0, 16),), jnp.float32)
    weight_up = scatter_about(splits[5], (D, 2 * FF), D ** -0.5, 0.25, ((0, 16),), jnp.float32)
    weight_down = scatter_about(splits[6], (FF, D), FF ** -0.5, 0.125, ((0, 16),), jnp.float32)
    norm_gains = jnp.clip(jax.random.uniform(splits[7], (GAINS,), jnp.float32, -0.15, 0.15) * levels(splits[7], (GAINS,), ((0, 16),), -0.4, 0.0), -0.15, 0.15)
    first_qkv = scatter_about(splits[8], (D, QKV), (0.0333 * (GROUPS * SEQ_LEN) ** 0.5), 40.0, ((0, 16),), jnp.float32)
    first_out = scatter_about(splits[9], (HEADS * HD, D), (0.111 * (GROUPS * SEQ_LEN) ** 0.5), 128.0, ((0, 16),), jnp.float32)
    first_up = scatter_about(splits[10], (D, 2 * FF), (0.0556 * (GROUPS * SEQ_LEN) ** 0.5), 80.0, ((0, 16),), jnp.float32)
    first_down = scatter_about(splits[11], (FF, D), (0.111 * (GROUPS * SEQ_LEN) ** 0.5), 128.0, ((0, 16),), jnp.float32)
    first_gains = scatter_about(splits[12], (GAINS,), (0.111 * (GROUPS * SEQ_LEN) ** 0.5), 128.0, ((0, 16),), jnp.float32)
    second_qkv = jnp.clip(jnp.exp(math.log(928.9728) - 1.3831247 * jax.random.uniform(splits[13], (D, QKV), jnp.float32) ** levels(splits[13], (D, QKV), ((0, 16),), -0.2, 0.2)), 232.98048, 928.9728)
    second_out = jnp.clip(jnp.exp(math.log(10321.92) - 1.3843914 * jax.random.uniform(splits[14], (HEADS * HD, D), jnp.float32) ** levels(splits[14], (HEADS * HD, D), ((0, 16),), -0.2, 0.2)), 2585.3953, 10321.92)
    second_up = jnp.clip(jnp.exp(math.log(2585.3953) - 1.3824993 * jax.random.uniform(splits[15], (D, 2 * FF), jnp.float32) ** levels(splits[15], (D, 2 * FF), ((0, 16),), -0.2, 0.2)), 648.8064, 2585.3953)
    second_down = jnp.clip(jnp.exp(math.log(10321.92) - 1.3843914 * jax.random.uniform(splits[16], (FF, D), jnp.float32) ** levels(splits[16], (FF, D), ((0, 16),), -0.2, 0.2)), 2585.3953, 10321.92)
    second_gains = jnp.clip(jnp.exp(math.log(10321.92) - 1.3843914 * jax.random.uniform(splits[17], (GAINS,), jnp.float32) ** levels(splits[17], (GAINS,), ((0, 16),), -0.2, 0.2)), 2585.3953, 10321.92)
    return {"tokens": tokens, "cotangent": cotangent, "positions": positions, "weight_qkv": weight_qkv, "weight_out": weight_out, "weight_up": weight_up, "weight_down": weight_down, "norm_gains": norm_gains, "first_qkv": first_qkv, "first_out": first_out, "first_up": first_up, "first_down": first_down, "first_gains": first_gains, "second_qkv": second_qkv, "second_out": second_out, "second_up": second_up, "second_down": second_down, "second_gains": second_gains}


NORM_EPS = 1e-06
ADAM_EPS = 1e-08
BETA_ONE = 0.9
BETA_TWO = 0.95
LEARN_RATE = 0.02
WEIGHT_DECAY = 0.1
ROPE_BASE = 10000.0
SCORE_SCALE = 0.0625
HIGHEST = lax.Precision.HIGHEST

@jax.custom_vjp
def low(v):
    return lax.optimization_barrier(v.astype(jnp.bfloat16)).astype(jnp.float32)

@jax.custom_vjp
def low_back(v):
    return v

def low_keep(v):
    return (low(v), None)

def low_pass(kept, grad):
    return (grad,)

def back_keep(v):
    return (v, None)

def back_low(kept, grad):
    return (low(grad),)
low.defvjp(low_keep, low_pass)
low_back.defvjp(back_keep, back_low)

def rms_norm(value, gain):
    scale = lax.rsqrt(lax.optimization_barrier(jnp.mean(value * value, axis=-1, keepdims=True)) + NORM_EPS)
    return value * scale * (1.0 + gain)

def rotary(value, cosine, sine):
    half_width = value.shape[-1] // 2
    lower = value[..., :half_width]
    upper = value[..., half_width:]
    return jnp.concatenate([lower * cosine - upper * sine, upper * cosine + lower * sine], axis=-1)

def tables(places):
    freqs = ROPE_BASE ** (-(jnp.arange(HD // 2) * 2.0 / HD))
    angle = places.astype(jnp.float32)[:, None] * freqs[None, :].astype(jnp.float32)
    return (jnp.cos(angle), jnp.sin(angle))

def window_mask(query_ids, key_ids, query_starts):
    later = key_ids[None, :] >= query_starts[:, None]
    causal = key_ids[None, :] <= query_ids[:, None]
    inside = query_ids[:, None] - key_ids[None, :] < WINDOW
    return later & causal & inside

def attend(queries, key_rows, values, starts):
    row_count = queries.shape[0]
    block_rows = min(row_count, 512)
    joined = jnp.concatenate([key_rows, values], axis=1)
    padded = jnp.concatenate([jnp.zeros((WINDOW, 2 * HD), joined.dtype), joined], axis=0)

    def one_block(block_index):
        first_row = block_index * block_rows
        block_query = lax.dynamic_slice_in_dim(queries, first_row, block_rows, 0)
        block_kv = lax.dynamic_slice_in_dim(padded, first_row, block_rows + WINDOW, 0)
        block_starts = lax.dynamic_slice_in_dim(starts, first_row, block_rows, 0)
        query_ids = first_row + jnp.arange(block_rows, dtype=jnp.int32)
        key_ids = first_row - WINDOW + jnp.arange(block_rows + WINDOW, dtype=jnp.int32)
        visible = window_mask(query_ids, key_ids, block_starts)
        scores = low_back(jnp.einsum('qhd,kd->hqk', block_query, block_kv[:, :HD], precision=HIGHEST) * SCORE_SCALE)
        scores = jnp.where(visible[None], scores, -1e+30)
        exponent = jnp.exp(scores - lax.optimization_barrier(jnp.max(scores, axis=-1, keepdims=True)))
        attention = low(exponent / lax.optimization_barrier(jnp.sum(exponent, axis=-1, keepdims=True)))
        mixed = jnp.einsum('hqk,kd->qhd', attention, block_kv[:, HD:], precision=HIGHEST)
        return mixed.reshape(block_rows, HEADS * HD)
    blocks = lax.map(jax.checkpoint(one_block), jnp.arange(row_count // block_rows, dtype=jnp.int32))
    return blocks.reshape(row_count, HEADS * HD)

def forward(inputs, copy_qkv, copy_out, copy_up, copy_down, copy_gains, cosine, sine, starts):
    gain_in = copy_gains[:D]
    gain_attn = copy_gains[D:2 * D]
    gain_pre = copy_gains[2 * D:3 * D]
    gain_post = copy_gains[3 * D:4 * D]
    gain_query = copy_gains[4 * D:4 * D + HD]
    gain_key = copy_gains[4 * D + HD:]
    row_count = inputs.shape[0]
    width_q = HEADS * HD
    normed_in = low(rms_norm(inputs, gain_in))
    projected = low_back(jnp.dot(normed_in, copy_qkv, precision=HIGHEST))
    raw_query = projected[:, :width_q].reshape(row_count, HEADS, HD)
    raw_key = projected[:, width_q:width_q + HD]
    raw_value = projected[:, width_q + HD:]
    queries = low(rotary(rms_norm(raw_query, gain_query), cosine[:, None, :], sine[:, None, :]))
    key_rows = low(rotary(rms_norm(raw_key, gain_key), cosine, sine))
    values = low(raw_value)
    context = low(low_back(attend(queries, key_rows, values, starts)))
    attn_raw = low_back(jnp.dot(context, copy_out, precision=HIGHEST))
    middle = inputs + rms_norm(attn_raw, gain_attn)
    normed_ff = low(rms_norm(middle, gain_pre))
    gate_up = low_back(jnp.dot(normed_ff, copy_up, precision=HIGHEST))
    hidden = low(jax.nn.gelu(gate_up[:, :FF], approximate=True) * gate_up[:, FF:])
    ffn_raw = low_back(jnp.dot(hidden, copy_down, precision=HIGHEST))
    return middle + rms_norm(ffn_raw, gain_post)

def adamw(weight, gradient, moment_one, moment_two, decay_rate):
    moment_one = BETA_ONE * moment_one + (1.0 - BETA_ONE) * gradient
    moment_two = BETA_TWO * moment_two + (1.0 - BETA_TWO) * gradient * gradient
    fix_one = 1.0 - BETA_ONE ** STEP
    fix_two = 1.0 - BETA_TWO ** STEP
    change = moment_one / fix_one / (jnp.sqrt(moment_two / fix_two) + ADAM_EPS) + decay_rate * weight
    return (weight - LEARN_RATE * change, moment_one, moment_two)

def reference(tokens, cotangent, positions, weight_qkv, weight_out, weight_up, weight_down, norm_gains, first_qkv, first_out, first_up, first_down, first_gains, second_qkv, second_out, second_up, second_down, second_gains):
    masters = (weight_qkv, weight_out, weight_up, weight_down, norm_gains)
    copies = tuple((low(weight) for weight in masters))

    def one_group(carry, item):
        group_tokens, group_back, group_places = item
        cosine, sine = tables(group_places)
        starts = jnp.arange(SEQ_LEN, dtype=jnp.int32) - group_places

        def layer(inputs, *weights):
            return forward(inputs, *weights, cosine, sine, starts)
        outputs, pull = jax.vjp(layer, group_tokens.astype(jnp.float32), *copies)
        gradients = pull(group_back.astype(jnp.float32))
        carry = tuple((running + gradient for running, gradient in zip(carry, gradients[1:])))
        return (carry, (outputs.astype(jnp.bfloat16), gradients[0]))
    initial = tuple((jnp.zeros_like(weight) for weight in masters))
    totals, (output_tokens, grad_tokens) = lax.scan(one_group, initial, (tokens, cotangent, positions))
    new_qkv, mean_qkv, square_qkv = adamw(weight_qkv, totals[0], first_qkv, second_qkv, WEIGHT_DECAY)
    new_out, mean_out, square_out = adamw(weight_out, totals[1], first_out, second_out, WEIGHT_DECAY)
    new_up, mean_up, square_up = adamw(weight_up, totals[2], first_up, second_up, WEIGHT_DECAY)
    new_down, mean_down, square_down = adamw(weight_down, totals[3], first_down, second_down, WEIGHT_DECAY)
    new_gains, mean_gains, square_gains = adamw(norm_gains, totals[4], first_gains, second_gains, 0.0)
    return (output_tokens, grad_tokens, new_qkv, new_out, new_up, new_down, new_gains, mean_qkv, mean_out, mean_up, mean_down, mean_gains, square_qkv, square_out, square_up, square_down, square_gains)
```

```python
import jax
import numpy as np
import jax.numpy as jnp
from jax import lax
from jax.experimental import pallas as pl
from jax.experimental.pallas import tpu as pltpu
from jax.sharding import PartitionSpec as P

D = 640
FF = 2048
HEADS = 4
HD = 256
WINDOW = 512
STEP = 10


NORM_EPS = 1e-06
ADAM_EPS = 1e-08
BETA_ONE = 0.9
BETA_TWO = 0.95
LEARN_RATE = 0.02
WEIGHT_DECAY = 0.1
ROPE_BASE = 10000.0
SCORE_SCALE = 0.0625
MESH = pl.DeviceIdType.MESH


def tables():
    return np.float32(ROPE_BASE ** (-(np.arange(HD // 2) * 2.0 / HD)))[None]


def adamw(weight, gradient, moment_one, moment_two, decay_rate):
    moment_one = BETA_ONE * moment_one + (1.0 - BETA_ONE) * gradient
    moment_two = BETA_TWO * moment_two + (1.0 - BETA_TWO) * gradient * gradient
    fix_one = 1.0 - BETA_ONE**STEP
    fix_two = 1.0 - BETA_TWO**STEP
    change = (
        moment_one / fix_one / (jnp.sqrt(moment_two / fix_two) + ADAM_EPS) + decay_rate * weight
    )
    return (weight - LEARN_RATE * change, moment_one, moment_two)


class Place:
    def __init__(self):
        seq = lax.axis_index("seq")
        shard = lax.axis_index("shard")
        self.x = lax.rem(seq, 4)
        self.zl = seq // 4
        self.y = lax.axis_index("batch")
        self.zh = shard // 2
        self.c = lax.rem(shard, 2)
        self.xp, self.xm, self.x2 = (lax.rem(self.x + k, 4) for k in (1, 3, 2))
        self.yp, self.ym, self.y2 = (lax.rem(self.y + k, 4) for k in (1, 3, 2))
        self.sib = self.at()
        self.sib["shard"] = self.zh * 2 + 1 - self.c
        self.to_xp, self.to_xm = self.at(x=self.xp), self.at(x=self.xm)
        self.to_yp, self.to_ym = self.at(y=self.yp), self.at(y=self.ym)
        self.to_zf = self.at(zl=1 - self.zl)
        self.to_zq = self.at(zl=1 - self.zl, zh=1 - self.zh)
        self.to_x2, self.to_y2 = self.at(x=self.x2), self.at(y=self.y2)
        self.to_z2 = self.at(zh=1 - self.zh)
        self.sib_zf = self.at(zl=1 - self.zl)
        self.sib_zf["shard"] = self.sib["shard"]

        for name, step in (("next", 1), ("next2", 2), ("prev", 7), ("prev2", 6)):
            there = self.at()
            there["seq"] = lax.rem(seq + step, 8)
            setattr(self, "to_" + name, there)

    def at(self, x=None, y=None, zl=None, zh=None):
        x = self.x if x is None else x
        y = self.y if y is None else y
        zl = self.zl if zl is None else zl
        zh = self.zh if zh is None else zh
        return {"seq": zl * 4 + x, "batch": y, "shard": zh * 2 + self.c}

    def neighbours(self):
        return (self.sib, self.to_xp, self.to_xm, self.to_yp, self.to_ym, self.to_zf, self.to_zq) + (
            self.to_next, self.to_next2, self.to_prev, self.to_prev2,
            self.to_x2, self.to_y2, self.to_z2, self.sib_zf,
        )


def greet(place):
    barrier = pltpu.get_barrier_semaphore()
    near = place.neighbours()
    for device in near:
        pl.semaphore_signal(barrier, inc=1, device_id=device, device_id_type=MESH)
    pl.semaphore_wait(barrier, len(near))


class Wire:
    def __init__(self, send_sems, recv_sems):
        self.send_sems, self.recv_sems, self.copies = send_sems, recv_sems, []

    def send(self, src, dst, device):
        number = len(self.copies)
        copy = pltpu.make_async_remote_copy(
            src_ref=src,
            dst_ref=dst,
            send_sem=self.send_sems.at[number],
            recv_sem=self.recv_sems.at[number],
            device_id=device,
            device_id_type=MESH,
        )
        copy.start()
        self.copies.append(copy)
        return copy

    def same(self, ref, device):
        return self.send(ref, ref, device)

    def drain(self):
        for copy in self.copies:
            copy.wait_send()


def cols(start, size):
    return pl.ds(pl.multiple_of(start, 128), size)


def rows(start, size, unit=16):
    return pl.ds(pl.multiple_of(start, unit), size)


COPIES = 192


def dot(left, right):
    return jnp.dot(left, right, preferred_element_type=jnp.float32)


def dot_nt(left, right):
    return lax.dot_general(left, right, (((1,), (1,)), ((), ())), preferred_element_type=jnp.float32)


def dot_tn(left, right):
    return lax.dot_general(left, right, (((0,), (0,)), ((), ())), preferred_element_type=jnp.float32)


def scale_of(value):
    return lax.rsqrt(jnp.mean(value * value, axis=-1, keepdims=True) + NORM_EPS)


def norm_back(grad, value, scale, gain):
    spread = gain * grad
    inner = jnp.mean(spread * value, axis=-1, keepdims=True)
    d_value = scale * spread - value * (scale * scale * scale * inner)
    d_gain = jnp.sum(grad * (value * scale), axis=0, keepdims=True)
    return d_value, d_gain


def turn(value, cosine, sine):
    lower, upper = value[:, :128], value[:, 128:]
    return jnp.concatenate([lower * cosine - upper * sine, upper * cosine + lower * sine], axis=1)


def turn_back(value, cosine, sine):
    lower, upper = value[:, :128], value[:, 128:]
    return jnp.concatenate([lower * cosine + upper * sine, upper * cosine - lower * sine], axis=1)


def gelu_parts(gate):
    root = 0.7978845608028654
    inner = jnp.tanh(root * (gate + 0.044715 * gate * gate * gate))
    half = 0.5 * (1.0 + inner)
    slope = half + 0.5 * gate * (1.0 - inner * inner) * (root * (1.0 + 3 * 0.044715 * gate * gate))
    return gate * half, slope


def low_add(*terms):
    total = terms[0].astype(jnp.float32)
    for term in terms[1:]:
        total = total + term.astype(jnp.float32)
    return total


def layer_kernel(
    tok_hbm, cot_hbm, place_ref, freq_ref, qkv_hbm, out_hbm, up_hbm, down_hbm, gain_ref,
    y_ref, dx_ref, rq, rk, ro, ru, rd, tg,
    tok_ref, cot_ref, place_col, cos_ref, sin_ref, k_in, q_in, u_in, o_in, d_in, in_sems,
    q_all, k_all, o_all, u_all, d_all, q_near, k_near, u_near, gn_c, gn_z, gn_y, gain_all,
    nin, proj, qkv_scale, qs, kv, probs, ctx, raw, mid, ffl, act, hid_x, gc_query,
    df, dg_x, d_ctx, d_kv, kv_out, kv_in1, kv_in2, fft,
    go, co, hu, hq, hk, ho, hd,
    ux1, ux2, su_, uy1, uy2, tu, uz1,
    qy1, qy2, tq, qz1, qx,
    ky1, ky2, tk, kz1, kx,
    oy1, oy2, to, oz1, ox,
    dz1, dz2, sd_, dy1, dy2, dxx,
    gc, gz, gy, gx,
    send_sems, recv_sems,
):
    low, f32 = jnp.bfloat16, jnp.float32
    p = Place()
    x, y, zl, zh, c = p.x, p.y, p.zl, p.zh, p.c
    zo, lo = 1 - zh, 1 - zl
    z, z2 = zh * 2 + zl, zo * 2 + zl
    zf, zq = zh * 2 + lo, zo * 2 + lo
    slot_one, slot_two = 2 * c, 2 - c
    dq_x, dk_x = act.at[:, :, 0:512], act.at[:, :, 512:768]

    def u_part(ax):
        return cols(c * 2048 + 512 * ax, 512)

    q_half, k_half = cols(c * 512, 512), cols(c * 256, 256)
    fetches = []
    for src, dst in (
        (qkv_hbm.at[:, cols(1024 + c * 256, 256)], k_in), (qkv_hbm.at[:, q_half], q_in),
        (up_hbm.at[:, u_part(x)], u_in), (out_hbm, o_in),
        (down_hbm, d_in), (tok_hbm, tok_ref), (cot_hbm, cot_ref),
    ):
        fetch = pltpu.make_async_copy(src, dst, in_sems.at[len(fetches)])
        fetch.start()
        fetches.append(fetch)
    greet(p)
    wire = Wire(send_sems, recv_sems)

    def recv(*copies):
        for copy in copies:
            copy.wait_recv()

    gn_c[0] = gain_ref[...]
    near_k = wire.send(qkv_hbm.at[:, cols(1280 - c * 256, 256)], k_near, p.sib)
    near_q = wire.send(qkv_hbm.at[:, cols((1 - c) * 512, 512)], q_near, p.sib)
    near_u = wire.send(up_hbm.at[:, cols((1 - c) * 2048 + 512 * x, 512)], u_near, p.sib)
    near_g = wire.send(gn_c.at[0], gn_c.at[1], p.sib)

    def pair(mine, other):
        first = jnp.where(c == 0, mine, other)
        second = jnp.where(c == 0, other, mine)
        return jnp.concatenate([first, second], axis=0).astype(low)

    fetches[0].wait()
    recv(near_k)
    k_all[y, zh, :, k_half] = pair(k_in[...], k_near[...])
    own_k = k_all.at[y, zh, :, k_half]
    kz = wire.same(own_k, p.to_zq)
    k1 = [wire.same(own_k, p.to_yp), wire.same(own_k, p.to_ym)]
    fetches[1].wait()
    recv(near_q)
    q_all[y, zh, :, q_half] = pair(q_in[...], q_near[...])
    own_q = q_all.at[y, zh, :, q_half]
    qz = wire.same(own_q, p.to_zq)
    q1 = [wire.same(own_q, p.to_yp), wire.same(own_q, p.to_ym)]
    fetches[2].wait()
    recv(near_u)
    u_all[y, zh, :, u_part(x)] = pair(u_in[...], u_near[...])
    own_u = u_all.at[y, zh, :, u_part(x)]
    uz = wire.same(own_u, p.to_zq)
    u1 = [wire.same(own_u, p.to_yp), wire.same(own_u, p.to_ym)]
    recv(near_g)
    gn_z[0] = gn_c[0] + gn_c[1]
    gzc = wire.send(gn_z.at[0], gn_z.at[1], p.to_zq)
    for fetch in fetches[3:]:
        fetch.wait()
    o_all[y, zh, c] = o_in[...].astype(low)
    d_all[y, zh, c] = d_in[...].astype(low)
    own_o, own_d = o_all.at[y, zh, c], d_all.at[y, zh, c]
    recv(kz)
    k2 = [wire.same(k_all.at[y, zo, :, k_half], to_) for to_ in (p.to_yp, p.to_ym)]
    recv(qz)
    q2 = [wire.same(q_all.at[y, zo, :, q_half], to_) for to_ in (p.to_yp, p.to_ym)]
    recv(uz)
    u2 = [wire.same(u_all.at[y, zo, :, u_part(x)], to_) for to_ in (p.to_yp, p.to_ym)]

    def round_x(k):
        piece = u_all.at[k, :, :, u_part(x)]
        return [wire.same(piece, p.to_xp), wire.same(piece, p.to_xm)]

    u4 = [round_x(y)]
    recv(gzc)
    gn_y[y] = gn_z[0] + gn_z[1]
    g2 = [wire.same(gn_y.at[y], to_) for to_ in (p.to_yp, p.to_ym, p.to_y2)]

    inputs = tok_ref[...].astype(f32)
    raw[...] = inputs * scale_of(inputs)
    for r in range(3):
        here = slice(128 * r, 128 * (r + 1))
        place = jnp.broadcast_to(place_ref[r : r + 1].astype(f32), (128, 128)).T
        place_col[here] = place
        angle = place * freq_ref[...]
        cos_ref[here] = jnp.cos(angle)
        sin_ref[here] = jnp.sin(angle)

    recv(k1[0])
    k3a = wire.same(k_all.at[p.ym, zh, :, k_half], p.to_yp)
    recv(k2[1])
    k3b = wire.same(k_all.at[p.yp, zo, :, k_half], p.to_ym)
    recv(k1[1], k2[0])
    sib_k = [wire.same(k_all.at[k, :, :, k_half], p.sib) for k in (y, p.ym, p.yp)]
    recv(q1[0])
    q3a = wire.same(q_all.at[p.ym, zh, :, q_half], p.to_yp)
    recv(q2[1])
    q3b = wire.same(q_all.at[p.yp, zo, :, q_half], p.to_ym)
    recv(u1[0])
    u3a = wire.same(u_all.at[p.ym, zh, :, u_part(x)], p.to_yp)
    recv(u2[1])
    u3b = wire.same(u_all.at[p.yp, zo, :, u_part(x)], p.to_ym)
    recv(k3a, k3b)
    sib_k.append(wire.same(k_all.at[p.y2, :, :, k_half], p.sib))
    recv(q1[1], q2[0])
    sib_q = [wire.same(q_all.at[k, :, :, q_half], p.sib) for k in (y, p.ym, p.yp)]
    recv(u1[1], u2[0])
    u4 += [round_x(p.ym), round_x(p.yp)]
    recv(*g2)
    gain_all[...] = 1.0 + ((gn_y[0] + gn_y[1]) + (gn_y[2] + gn_y[3]))
    oz = wire.same(own_o, p.to_zq)
    o1 = [wire.same(own_o, p.to_yp), wire.same(own_o, p.to_ym)]

    def gain_row(first, count):
        return jnp.concatenate([gain_all[k : k + 1] for k in range(first, first + count)], axis=1)

    def put_gain(first, grad):
        for k in range(grad.shape[1] // 128):
            gc[1, first + k : first + k + 1] = grad[:, 128 * k : 128 * (k + 1)]

    nin[c] = (raw[...] * gain_row(0, 5)).astype(low)
    nin_c = wire.same(nin.at[c], p.sib)
    u5 = []

    def pass_x(number):
        recv(u4[number][1])
        k = (y, p.ym, p.yp, p.y2)[number]
        u5.append(wire.same(u_all.at[k, :, :, u_part(p.xp)], p.to_xm))

    recv(*sib_k)

    cosine, sine = cos_ref[...], sin_ref[...]
    kv_raw = dot(nin[c], k_all[...].reshape(D, 512))
    proj[:, 1024:1280] = kv_raw[:, :HD]
    key_scale = scale_of(kv_raw[:, :HD])
    qkv_scale[:, 4:5] = key_scale
    kv[512:896, :HD] = turn(kv_raw[:, :HD] * key_scale * gain_row(22, 2), cosine, sine).astype(low)
    kv[512:896, HD:] = kv_raw[:, HD:].astype(low)
    kv_c1 = wire.send(kv.at[512:896], kv.at[128:512], p.to_next)
    kv_c2 = wire.send(kv.at[768:896], kv.at[0:128], p.to_next2)

    recv(u3a, u3b)
    u4.append(round_x(p.y2))
    sib_u = [wire.same(u_all.at[:, :, :, u_part(x)], p.sib)]
    recv(q3a, q3b)
    sib_q.append(wire.same(q_all.at[p.y2, :, :, q_half], p.sib))
    pass_x(0)
    recv(oz)
    o2 = [wire.same(o_all.at[y, zo, c], to_) for to_ in (p.to_yp, p.to_ym)]
    d1 = [wire.same(own_d, p.to_yp), wire.same(own_d, p.to_ym)]
    recv(o1[0])
    o3a = wire.same(o_all.at[p.ym, zh, c], p.to_yp)
    pass_x(1)
    recv(o2[1])
    o3b = wire.same(o_all.at[p.yp, zo, c], p.to_ym)
    recv(o1[1], o2[0])
    sib_o = [wire.same(o_all.at[k, :, c], p.sib) for k in (y, p.ym, p.yp)]
    recv(*sib_q)

    for h in range(HEADS):
        head = dot(nin[c], q_all[:, :, :, HD * h : HD * (h + 1)].reshape(D, HD))
        proj[:, HD * h : HD * (h + 1)] = head
        head_scale = scale_of(head)
        qkv_scale[:, h : h + 1] = head_scale
        qs[h] = turn(head * head_scale * gain_row(20, 2), cosine, sine).astype(low)

    recv(*d1)
    d3 = [
        wire.same(d_all.at[p.ym, zh, c, 0:64], p.to_yp),
        wire.same(d_all.at[p.yp, zh, c, 64:128], p.to_ym),
    ]
    pass_x(2)

    recv(kv_c1, kv_c2)
    row = lax.broadcasted_iota(jnp.int32, (128, 640), 0)
    column = lax.broadcasted_iota(jnp.int32, (128, 640), 1)
    distance = (row + 512 - column).astype(f32)
    for r in range(3):
        block_q = qs[:, 128 * r : 128 * (r + 1)].reshape(512, HD)
        block_kv = kv.at[128 * r : 128 * r + 640]
        furthest = jnp.minimum(place_col[128 * r : 128 * (r + 1), 0:1], WINDOW - 1.0)
        visible = (distance >= 0) & (distance <= furthest)
        scores = dot_nt(block_q, block_kv[:, :HD]).reshape(HEADS, 128, 640) * SCORE_SCALE
        scores = jnp.where(visible[None], scores, -1e30).reshape(512, 640)
        exponent = jnp.exp(scores - jnp.max(scores, axis=-1, keepdims=True))
        share = exponent * (1.0 / jnp.sum(exponent, axis=-1, keepdims=True))
        share = share.astype(low)
        probs[r] = share
        mixed = dot(share, block_kv[:, HD:])
        for h in range(HEADS):
            ctx[128 * r : 128 * (r + 1), HD * h : HD * (h + 1)] = mixed[
                128 * h : 128 * (h + 1)
            ].astype(low)
        if r == 0:
            pass_x(3)
            recv(o3a, o3b)
            sib_o.append(wire.same(o_all.at[p.y2, :, c], p.sib))
        if r == 1:
            sib_u.append(wire.same(u_all.at[:, :, :, u_part(p.xp)], p.sib))
            recv(*d3)
            d4 = wire.same(d_all.at[rows(2 * zl, 2, 2), zh, c], p.to_zq)
            sib_d = [wire.same(d_all.at[:, zh, c], p.sib)]

    recv(*sib_o)
    attn_raw = dot(ctx[...], o_all[...].reshape(HEADS * HD, D))
    raw[...] = attn_raw
    attn_scale = scale_of(attn_raw)
    qkv_scale[:, 5 : 5 + 1] = attn_scale
    middle = tok_ref[...].astype(f32) + attn_raw * attn_scale * gain_row(5, 5)
    mid[...] = middle
    mid_scale = scale_of(middle)
    qkv_scale[:, 6 : 6 + 1] = mid_scale
    ffl[c] = (middle * mid_scale * gain_row(10, 5)).astype(low)
    ffl_c = wire.same(ffl.at[c], p.sib)

    recv(d4)
    d5 = wire.same(d_all.at[rows(2 - 2 * zl, 2, 2), zo, c], p.to_zf)
    sib_d.append(wire.same(d_all.at[rows(2 - 2 * zl, 2, 2), zo, c], p.sib))
    recv(*[piece[0] for piece in u4])
    sib_u.append(wire.same(u_all.at[:, :, :, u_part(p.xm)], p.sib))

    def act_cols(k):
        return cols(256 * lax.rem(k, 6), 256)

    def up_step(i, quarter):
        k = 2 * quarter + i
        part = cols(256 * k, 256)
        gate = dot(ffl[c], u_all[:, :, :, part].reshape(D, 256))
        up = dot(ffl[c], u_all[:, :, :, cols(FF + 256 * k, 256)].reshape(D, 256))
        value, slope = gelu_parts(gate)
        act[k // 6, :, act_cols(k)] = value.astype(low)
        act[(k + 8) // 6, :, act_cols(k + 8)] = (up * slope).astype(low)
        hidden = (value * up).astype(low)
        hu[0:384, part] = hidden
        hid_x[k, slot_one] = hidden[:, :128]
        hid_x[k, slot_two] = hidden[:, 128:]
        return quarter

    for n, quarter in enumerate((x, p.xp, p.xm, p.x2)):
        if n == 3:
            recv(d5)
            sib_d.append(wire.same(d_all.at[rows(2 * zl, 2, 2), zo, c], p.sib))
            recv(*u5)
            sib_u.append(wire.same(u_all.at[:, :, :, u_part(p.x2)], p.sib))
        recv(sib_u[n])
        lax.fori_loop(0, 2, up_step, quarter)
    hid_c = wire.send(hid_x.at[:, 2], hid_x.at[:, c], p.sib)
    recv(*sib_d)
    ffn_raw = dot(hu[0:384], d_all[...].reshape(FF, D))
    ffn_scale = scale_of(ffn_raw)
    y_ref[...] = (mid[...] + ffn_raw * ffn_scale * gain_row(15, 5)).astype(low)

    d_ffn, dg_post = norm_back(cot_ref[...].astype(f32), ffn_raw, ffn_scale, gain_row(15, 5))
    put_gain(15, dg_post)
    df[c] = d_ffn.astype(low)
    df_c = wire.same(df.at[c], p.sib)

    def hidden_back(i, quarter):
        k = 2 * quarter + i
        part = cols(256 * k, 256)
        d_hidden = dot_nt(df[c], d_all[quarter, i].reshape(256, D))
        slope = act[(k + 8) // 6, :, act_cols(k + 8)].astype(f32)
        dg_x[slot_one, :, part] = (d_hidden * slope).astype(low)
        value = act[k // 6, :, act_cols(k)].astype(f32)
        dg_x[slot_two, :, part] = (d_hidden * value).astype(low)
        return quarter

    quarters = (p.x2, p.xp, p.xm, x)
    dg_c = []
    for quarter in quarters:
        lax.fori_loop(0, 2, hidden_back, quarter)
        part = cols(512 * quarter, 512)
        dg_c.append(wire.send(dg_x.at[2, :, part], dg_x.at[c, :, part], p.sib))
    recv(ffl_c)
    fft[...] = ffl[...].reshape(768, D).T

    def up_grad(n):
        recv(dg_c[n])
        part = cols(512 * quarters[n], 512)
        block = dot(fft[...], dg_x[0:2, :, part].reshape(768, 512))
        hu[:, part] = block.astype(low)

    up_grad(0)
    u_x1 = [
        wire.send(hu.at[:, cols(512 * p.x2, 256)], ux1.at[0], p.to_xm),
        wire.send(hu.at[:, cols(512 * p.x2 + 256, 256)], ux1.at[1], p.to_xp),
    ]
    up_grad(1)
    up_grad(2)
    recv(hid_c, df_c)

    def down_grad(k, _):
        block = dot_tn(hid_x[k, 0:2].reshape(768, 128), df[...].reshape(768, D))
        hd[k // 2, lax.rem(k, 2)] = block.reshape(2, 64, D).astype(low)
        return 0

    lax.fori_loop(0, 8, down_grad, 0)
    d_z1 = [
        wire.send(hd.at[0:2, zo, zl], dz1.at[0], p.to_zq),
        wire.send(hd.at[2:4, zo, zl], dz1.at[1], p.to_zf),
    ]
    up_grad(3)
    recv(*u_x1)

    def add_ux(k, _):
        here = rows(80 * k, 80)
        one, two = cols(512 * p.xm, 256), cols(512 * p.xp + 256, 256)
        hu[here, one] = low_add(hu[here, one], ux1[0, here]).astype(low)
        hu[here, two] = low_add(hu[here, two], ux1[1, here]).astype(low)
        return 0

    lax.fori_loop(0, 8, add_ux, 0)
    u_x2 = [
        wire.send(hu.at[:, cols(512 * p.xm, 512)], ux2.at[0], p.to_xm),
        wire.send(hu.at[:, cols(512 * p.xp, 512)], ux2.at[1], p.to_xp),
    ]
    recv(*d_z1)
    hd[0:2, zh, lo] = low_add(hd[0:2, zh, lo], dz1[0]).astype(low)
    hd[2:4, zo, lo] = low_add(hd[2:4, zo, lo], dz1[1]).astype(low)
    d_z2 = [
        wire.send(hd.at[:, zh, lo], dz2.at[0], p.to_zf),
        wire.send(hd.at[:, zo, lo], dz2.at[1], p.to_zq),
    ]
    d_normed = dot_nt(dg_x[slot_one], u_all[:, :, :, :FF].reshape(D, FF)) + dot_nt(
        dg_x[slot_two], u_all[:, :, :, FF:].reshape(D, FF)
    )
    d_middle, dg_pre = norm_back(d_normed, mid[...], qkv_scale[:, 6 : 6 + 1], gain_row(10, 5))
    put_gain(10, dg_pre)
    d_middle = d_middle + cot_ref[...].astype(f32)
    dx_ref[...] = d_middle
    d_attn, dg_attn = norm_back(d_middle, raw[...], qkv_scale[:, 5 : 5 + 1], gain_row(5, 5))
    put_gain(5, dg_attn)
    d_attn = d_attn.astype(low)
    d_ctx[...] = dot_nt(d_attn, o_all[...].reshape(HEADS * HD, D)).astype(low)
    go[...] = dot_tn(ctx[...], d_attn).astype(low).reshape(4, 2, 2, 64, D)
    o_c = wire.send(go.at[:, :, 1 - c], co, p.sib)

    recv(*d_z2)
    for k in range(4):
        sd_[k] = low_add(hd[k, zh, zl], dz2[0, k], dz2[1, k]).astype(low)
    d_y1 = [
        wire.send(sd_.at[p.y2, 0:32], dy1.at[0], p.to_ym),
        wire.send(sd_.at[p.y2, 32:64], dy1.at[1], p.to_yp),
    ]

    def add_us(k, _):
        i, j = k // 2, lax.rem(k, 2)
        here, part = rows(80 * k, 80), cols(512 * x, 512)
        su_[i, j] = low_add(hu[here, part], ux2[0, here], ux2[1, here]).astype(low)
        return 0

    d_kv[...] = jnp.zeros_like(d_kv)
    gc_query[...] = jnp.zeros((1, HD), f32)
    kv_b = []
    for r in range(3):
        here = slice(128 * r, 128 * (r + 1))
        span = slice(128 * r, 128 * r + 640)
        d_mixed = jnp.concatenate(
            [d_ctx[here, HD * h : HD * (h + 1)] for h in range(HEADS)], axis=0
        )
        share = probs[r].astype(f32)
        d_share = dot_nt(d_mixed, kv[span, HD:])
        d_scores = share * (d_share - jnp.sum(share * d_share, axis=-1, keepdims=True))
        d_scores = d_scores.astype(low)
        block_q = qs[:, here].reshape(512, HD)
        d_kv[span, :HD] += dot_tn(d_scores, block_q) * SCORE_SCALE
        d_kv[span, HD:] += dot_tn(probs[r], d_mixed)
        if r == 0:
            kv_out[0:128] = d_kv[0:128].astype(low)
            kv_b.append(wire.send(kv_out.at[0:128], kv_in2, p.to_prev2))
        if r == 1:
            kv_out[128:256] = d_kv[128:256].astype(low)
            kv_b.append(wire.send(kv_out.at[128:256], kv_in1.at[0:128], p.to_prev))
        if r == 2:
            kv_out[256:512] = d_kv[256:512].astype(low)
            kv_b.append(wire.send(kv_out.at[256:512], kv_in1.at[128:384], p.to_prev))
        d_query = dot(d_scores, kv[span, :HD]) * SCORE_SCALE
        for h in range(HEADS):
            piece = turn_back(d_query[128 * h : 128 * (h + 1)], cos_ref[here], sin_ref[here])
            d_head, d_gain = norm_back(
                piece, proj[here, HD * h : HD * (h + 1)], qkv_scale[here, h : h + 1], gain_row(20, 2)
            )
            gc_query[...] += d_gain
            slot, start = (slot_one, slot_two)[h // 2], HD * (h % 2)
            dq_x[slot, here, start : start + HD] = d_head.astype(low)
        if r == 0:
            recv(o_c)
            for i in range(4):
                for j in range(2):
                    ho[i, j] = low_add(go[i, j, c], co[i, j]).astype(low)
            o_y1 = [
                wire.send(ho.at[p.y2, 0], oy1.at[0], p.to_ym),
                wire.send(ho.at[p.y2, 1], oy1.at[1], p.to_yp),
            ]
        if r == 1:
            recv(*d_y1)
            sd_[p.ym, 0:32] = low_add(sd_[p.ym, 0:32], dy1[0]).astype(low)
            sd_[p.yp, 32:64] = low_add(sd_[p.yp, 32:64], dy1[1]).astype(low)
            d_y2 = [
                wire.send(sd_.at[p.ym], dy2.at[0], p.to_ym),
                wire.send(sd_.at[p.yp], dy2.at[1], p.to_yp),
            ]
            recv(*o_y1)
            ho[p.ym, 0] = low_add(ho[p.ym, 0], oy1[0]).astype(low)
            ho[p.yp, 1] = low_add(ho[p.yp, 1], oy1[1]).astype(low)
            o_y2 = [
                wire.send(ho.at[p.ym], oy2.at[0], p.to_ym),
                wire.send(ho.at[p.yp], oy2.at[1], p.to_yp),
            ]

        if r == 1:
            recv(*u_x2)
            lax.fori_loop(0, 8, add_us, 0)
            u_y1 = [
                wire.send(su_.at[p.y2, 0], uy1.at[0], p.to_ym),
                wire.send(su_.at[p.y2, 1], uy1.at[1], p.to_yp),
            ]

    dq_c = wire.send(dq_x.at[2], dq_x.at[c], p.sib)
    recv(*u_y1)
    su_[p.ym, 0] = low_add(su_[p.ym, 0], uy1[0]).astype(low)
    su_[p.yp, 1] = low_add(su_[p.yp, 1], uy1[1]).astype(low)
    u_y2 = [
        wire.send(su_.at[p.ym], uy2.at[0], p.to_ym),
        wire.send(su_.at[p.yp], uy2.at[1], p.to_yp),
    ]
    recv(*d_y2)
    dxx[x] = low_add(sd_[y], dy2[0], dy2[1]).astype(low)
    d_x = [wire.same(dxx.at[x], to_) for to_ in (p.to_xp, p.to_xm, p.to_x2)]
    recv(*o_y2)
    for k in range(2):
        to[k] = low_add(ho[y, k], oy2[0, k], oy2[1, k]).astype(low)
    o_z = [
        wire.send(to.at[zh, rows(32 * lo, 32)], oz1.at[0], p.to_zf),
        wire.send(to.at[zo, rows(32 * lo, 32)], oz1.at[1], p.to_zq),
        wire.send(to.at[zo, rows(32 * zl, 32)], oz1.at[2], p.to_z2),
    ]
    recv(nin_c)
    fft[...] = nin[...].reshape(768, D).T
    recv(dq_c)
    hq[...] = dot(fft[...], dq_x[0:2].reshape(768, 512)).astype(low).reshape(4, 2, 80, 512)

    def y_first(sums, landing):
        return [
            wire.send(sums.at[p.y2, 0], landing.at[0], p.to_ym),
            wire.send(sums.at[p.y2, 1], landing.at[1], p.to_yp),
        ]

    def y_second(sums, landed, landing):
        sums[p.ym, 0] = low_add(sums[p.ym, 0], landed[0]).astype(low)
        sums[p.yp, 1] = low_add(sums[p.yp, 1], landed[1]).astype(low)
        return [
            wire.send(sums.at[p.ym], landing.at[0], p.to_ym),
            wire.send(sums.at[p.yp], landing.at[1], p.to_yp),
        ]

    def z_all(total, sums, landed, landing):
        width = landing.shape[-1]
        for k in range(2):
            total[k] = low_add(sums[y, k], landed[0, k], landed[1, k]).astype(low)
        return [
            wire.send(total.at[zh, :, cols(width * lo, width)], landing.at[0], p.to_zf),
            wire.send(total.at[zo, :, cols(width * lo, width)], landing.at[1], p.to_zq),
            wire.send(total.at[zo, :, cols(width * zl, width)], landing.at[2], p.to_z2),
        ]

    def x_all(parts, total, landed):
        width = landed.shape[-1]
        mine = total[zh, :, cols(width * zl, width)]
        parts[x] = low_add(mine, landed[0], landed[1], landed[2]).astype(low)
        return [wire.same(parts.at[x], to_) for to_ in (p.to_xp, p.to_xm, p.to_x2)]

    def to_readers(result, parts):
        width = parts.shape[-1]
        mine = cols(2 * width * c + width * zl, width)
        result[:, mine] = low_add(parts[0], parts[1], parts[2], parts[3]).astype(low)
        return [wire.same(result.at[:, mine], to_) for to_ in (p.to_zf, p.sib, p.sib_zf)]

    q_y1 = y_first(hq, qy1)
    recv(*u_y2)
    for k in range(2):
        tu[k] = low_add(su_[y, k], uy2[0, k], uy2[1, k]).astype(low)
    u_z = [
        wire.send(tu.at[zh, :, cols(256 * lo, 256)], uz1.at[0], p.to_zf),
        wire.send(tu.at[zo, :, cols(256 * lo, 256)], uz1.at[1], p.to_zq),
        wire.send(tu.at[zo, :, cols(256 * zl, 256)], uz1.at[2], p.to_z2),
    ]

    recv(*kv_b)
    d_key = d_kv[512:896] + kv_in1[...].astype(f32)
    tail = jnp.concatenate([jnp.zeros((256, 512), f32), kv_in2[...].astype(f32)], axis=0)
    d_key = d_key + tail
    dk_x[slot_two] = d_key[:, HD:].astype(low)
    piece = turn_back(d_key[:, :HD], cos_ref[...], sin_ref[...])
    d_head, dg_key = norm_back(
        piece, proj[:, 1024 : 1024 + HD], qkv_scale[:, 4:5], gain_row(22, 2)
    )
    put_gain(22, dg_key)
    dk_x[slot_one] = d_head.astype(low)
    dk_c = wire.send(dk_x.at[2], dk_x.at[c], p.sib)

    recv(*q_y1)
    q_y2 = y_second(hq, qy1, qy2)
    recv(dk_c)
    hk[...] = dot(fft[...], dk_x[0:2].reshape(768, 256)).astype(low).reshape(4, 2, 80, 256)
    k_y1 = y_first(hk, ky1)

    d_normed = dot_nt(dq_x[slot_one], q_all[:, :, :, :512].reshape(D, 512)) + dot_nt(
        dq_x[slot_two], q_all[:, :, :, 512:].reshape(D, 512)
    )
    d_normed = d_normed + dot_nt(dk_x[slot_one], k_all[:, :, :, :256].reshape(D, 256))
    d_normed = d_normed + dot_nt(dk_x[slot_two], k_all[:, :, :, 256:].reshape(D, 256))
    recv(*k_y1)
    k_y2 = y_second(hk, ky1, ky2)
    inputs = tok_ref[...].astype(f32)
    d_input, dg_in = norm_back(d_normed, inputs, scale_of(inputs), gain_row(0, 5))
    dx_ref[...] += d_input

    put_gain(0, dg_in)
    put_gain(20, gc_query[...])
    g_c = wire.send(gc.at[1], gc.at[0], p.sib)

    recv(*q_y2)
    q_z = z_all(tq, hq, qy2, qz1)
    recv(g_c)
    gz[z] = gc[0] + gc[1]
    g_z = [wire.same(gz.at[z], to_) for to_ in (p.to_zf, p.to_zq, p.to_z2)]
    recv(*o_z)
    ox[x] = low_add(to[zh, rows(32 * zl, 32)], oz1[0], oz1[1], oz1[2]).astype(low)
    o_x = [wire.same(ox.at[x], to_) for to_ in (p.to_xp, p.to_xm, p.to_x2)]
    recv(*d_x)
    rd[zl] = low_add(dxx[0], dxx[1], dxx[2], dxx[3]).astype(low)
    d_f = wire.same(rd.at[zl], p.to_zf)
    recv(*u_z)
    ru[c, zl, x] = low_add(tu[zh, :, cols(256 * zl, 256)], uz1[0], uz1[1], uz1[2]).astype(low)
    u_a = [wire.same(ru.at[c, zl, x], to_) for to_ in (p.to_xp, p.to_xm, p.to_x2)]
    recv(*g_z)
    gy[y] = (gz[0] + gz[1]) + (gz[2] + gz[3])
    g_y = [wire.same(gy.at[y], to_) for to_ in (p.to_yp, p.to_ym, p.to_y2)]
    recv(*k_y2)
    k_z = z_all(tk, hk, ky2, kz1)
    recv(*q_z)
    q_x = x_all(qx, tq, qz1)
    recv(*o_x)
    ro[zl] = low_add(ox[0], ox[1], ox[2], ox[3]).astype(low)
    o_f = wire.same(ro.at[zl], p.to_zf)
    recv(*u_a)
    u_b = [wire.same(ru.at[c, zl], to_) for to_ in (p.to_zf, p.sib, p.sib_zf)]
    recv(*g_y)
    gx[x] = (gy[0] + gy[1]) + (gy[2] + gy[3])
    g_x = [wire.same(gx.at[x], to_) for to_ in (p.to_xp, p.to_xm, p.to_x2)]
    recv(*k_z)
    k_x = x_all(kx, tk, kz1)
    recv(*q_x)
    q_f = to_readers(rq, qx)
    recv(*g_x)
    tg[...] = (gx[0] + gx[1]) + (gx[2] + gx[3])
    recv(*k_x)
    k_f = to_readers(rk, kx)
    recv(d_f, o_f, *u_b, *q_f, *k_f)
    wire.drain()


def layer(tokens, cotangent, places, weights, gains):
    low, f32 = jnp.bfloat16, jnp.float32
    owner = lax.axis_index("batch") * 4 + lax.axis_index("shard")
    own_gains = lax.dynamic_update_slice(
        jnp.zeros((3072,), f32), gains.astype(low).astype(f32), (owner * 192,)
    ).reshape(24, 128)

    def vm(*shape, kind=low):
        return pltpu.VMEM(shape, kind)

    spaces = [pl.ANY] * 2 + [pltpu.VMEM] * 2 + [pl.ANY] * 4 + [pltpu.VMEM]
    outs = [
        ((384, D), low), ((384, D), f32), ((80, 1024), low), ((80, 512), low), ((2, 32, D), low),
        ((2, 2, 4, 80, 256), low), ((2, 64, D), low), ((24, 128), f32),
    ]
    return pl.pallas_call(
        layer_kernel,
        out_shape=[jax.ShapeDtypeStruct(s, k) for s, k in outs],
        in_specs=[pl.BlockSpec(memory_space=space) for space in spaces],
        out_specs=[pl.BlockSpec(memory_space=pltpu.VMEM)] * 8,
        scratch_shapes=[
            vm(384, D), vm(384, D), vm(384, 128, kind=f32), vm(384, 128, kind=f32),
            vm(384, 128, kind=f32), vm(40, 256, kind=f32), vm(40, 512, kind=f32),
            vm(40, 512, kind=f32), vm(64, D, kind=f32), vm(128, D, kind=f32), pltpu.SemaphoreType.DMA((7,)),
            vm(4, 2, 80, 1024), vm(4, 2, 80, 512), vm(4, 2, 2, 64, D), vm(4, 2, 80, 4096), vm(4, 2, 2, 128, D),
            vm(40, 512, kind=f32), vm(40, 256, kind=f32), vm(40, 512, kind=f32),
            vm(2, 24, 128, kind=f32), vm(2, 24, 128, kind=f32), vm(4, 24, 128, kind=f32),
            vm(24, 128, kind=f32),
            vm(2, 384, D), vm(384, 1280, kind=f32), vm(384, 128, kind=f32), vm(4, 384, HD),
            vm(896, 512), vm(3, 512, 640), vm(384, 1024), vm(384, D, kind=f32),
            vm(384, D, kind=f32), vm(2, 384, D), vm(3, 384, 1536),
            vm(8, 3, 384, 128), vm(1, HD, kind=f32),
            vm(2, 384, D), vm(3, 384, FF), vm(384, 1024),
            vm(896, 512, kind=f32), vm(512, 512), vm(384, 512), vm(128, 512),
            vm(D, 768),
            vm(4, 2, 2, 64, D), vm(4, 2, 64, D),
            vm(D, 2048), vm(4, 2, 80, 512), vm(4, 2, 80, 256), vm(4, 2, 64, D), vm(4, 2, 2, 64, D),
            vm(2, D, 256), vm(2, D, 512), vm(4, 2, 80, 512),
            vm(2, 80, 512), vm(2, 2, 80, 512), vm(2, 80, 512),
            vm(3, 80, 256),
            vm(2, 80, 512), vm(2, 2, 80, 512), vm(2, 80, 512), vm(3, 80, 256), vm(4, 80, 256),
            vm(2, 80, 256), vm(2, 2, 80, 256), vm(2, 80, 256), vm(3, 80, 128), vm(4, 80, 128),
            vm(2, 64, D), vm(2, 2, 64, D), vm(2, 64, D),
            vm(3, 32, D), vm(4, 32, D),
            vm(2, 2, 64, D), vm(2, 4, 64, D), vm(4, 64, D),
            vm(2, 32, D), vm(2, 64, D), vm(4, 64, D),
            vm(2, 24, 128, kind=f32), vm(4, 24, 128, kind=f32),
            vm(4, 24, 128, kind=f32), vm(4, 24, 128, kind=f32),
            pltpu.SemaphoreType.DMA((COPIES,)),
            pltpu.SemaphoreType.DMA((COPIES,)),
        ],
        compiler_params=pltpu.CompilerParams(
            collective_id=0, has_side_effects=True, vmem_limit_bytes=62 * 1024 * 1024
        ),
        name="layer",
    )(tokens, cotangent, places, tables(), *weights, own_gains)


SHAPES = [(40, 1536), (64, D), (40, 4096), (128, D)]


def adam_kernel(*refs):
    dx_hbm, y_hbm, rk_hbm = refs[:3]
    ins, (dx_out, y_out), outs = refs[3:19], refs[19:21], refs[21:33]
    held, made, (dx_vm, y_vm, rk_vm) = refs[33:49], refs[49:61], refs[61:64]
    in_sems, out_sems, pass_sems = refs[64:]
    c = lax.rem(lax.axis_index("shard"), 2)
    order = (0, 1, 3, 2)
    fetches, stores = {}, []
    for k in order:
        for n in range(4 * k, 4 * k + 4):
            fetches[n] = pltpu.make_async_copy(ins[n], held[n], in_sems.at[n])
            fetches[n].start()
    rest = [
        pltpu.make_async_copy(src, dst, pass_sems.at[n])
        for n, (src, dst) in enumerate(((rk_hbm, rk_vm), (dx_hbm, dx_vm), (y_hbm, y_vm)))
    ]
    for copy in rest:
        copy.start()

    def own_rows(total):
        total = total.astype(jnp.float32)
        return jnp.where(c == 0, total[:40], total[40:])

    for k in order:
        for n in range(4 * k, 4 * k + 4):
            fetches[n].wait()
        total, weight, one, two = held[4 * k : 4 * k + 4]
        new, mean, square = made[3 * k : 3 * k + 3]

        def adam_into(part, gradient):
            new[part], mean[part], square[part] = adamw(
                weight[part], gradient, one[part], two[part], WEIGHT_DECAY
            )

        if k == 0:
            rest[0].wait()
            adam_into((slice(None), slice(0, 1024)), own_rows(total[...]))
            adam_into((slice(None), slice(1024, 1536)), own_rows(rk_vm[...]))
        elif k == 2:
            for core in range(2):
                for ax in range(4):
                    for zl in range(2):
                        start = 2048 * core + 512 * ax + 256 * zl
                        adam_into(
                            (slice(None), slice(start, start + 256)),
                            own_rows(total[core, zl, ax]),
                        )
        else:
            height = total.shape[1]
            for n in range(2):
                adam_into(slice(height * n, height * (n + 1)), total[n].astype(jnp.float32))
        for n in range(3 * k, 3 * k + 3):
            stores.append(pltpu.make_async_copy(made[n], outs[n], out_sems.at[n]))
            stores[-1].start()
        if k == 3:
            for n, (src, dst) in enumerate(((dx_vm, dx_out), (y_vm, y_out))):
                rest[1 + n].wait()
                stores.append(pltpu.make_async_copy(src, dst, pass_sems.at[3 + n]))
                stores[-1].start()
    for copy in stores:
        copy.wait()


def update(dx, y, rk, totals, weights, firsts, seconds):
    f32 = jnp.float32
    ins = [a for k in range(4) for a in (totals[k], weights[k], firsts[k], seconds[k])]
    results = [jax.ShapeDtypeStruct(s, f32) for s in SHAPES for _ in range(3)]
    dx, y, *made = pl.pallas_call(
        adam_kernel,
        out_shape=[jax.ShapeDtypeStruct(a.shape, a.dtype) for a in (dx, y)] + results,
        in_specs=[pl.BlockSpec(memory_space=pl.ANY)] * 19,
        out_specs=[pl.BlockSpec(memory_space=pl.ANY)] * 14,
        scratch_shapes=[pltpu.VMEM(a.shape, a.dtype) for a in ins]
        + [pltpu.VMEM(a.shape, a.dtype) for a in results]
        + [pltpu.VMEM(a.shape, a.dtype) for a in (dx, y, rk)]
        + [pltpu.SemaphoreType.DMA((n,)) for n in (16, 12, 5)],
        compiler_params=pltpu.CompilerParams(vmem_limit_bytes=62 * 1024 * 1024),
        name="update",
    )(dx, y, rk, *ins)
    return (dx, y, *made[0::3], *made[1::3], *made[2::3])


def shards(
    tokens, cotangent, positions,
    weight_qkv, weight_out, weight_up, weight_down, norm_gains,
    first_qkv, first_out, first_up, first_down, first_gains,
    second_qkv, second_out, second_up, second_down, second_gains,
):
    weights = (weight_qkv, weight_out, weight_up, weight_down)
    y, dx, rq, rk, ro, ru, rd, tg = layer(
        tokens[0], cotangent[0], positions[0].reshape(3, 128), weights, norm_gains
    )
    dx, y, *results = update(
        dx, y, rk, (rq, ro, ru, rd), weights,
        (first_qkv, first_out, first_up, first_down),
        (second_qkv, second_out, second_up, second_down),
    )
    owner = lax.axis_index("batch") * 4 + lax.axis_index("shard")
    total_gains = lax.dynamic_slice_in_dim(tg.reshape(3072), owner * 192, 192)
    new_gains, mean_gains, square_gains = adamw(
        norm_gains, total_gains, first_gains, second_gains, 0.0
    )
    return (
        y[None], dx[None],
        *results[0:4], new_gains, *results[4:8], mean_gains, *results[8:12], square_gains,
    )


def solution(mesh):
    return jax.shard_map(
        shards,
        mesh=mesh,
        in_specs=(
            P(("batch", "shard"), "seq", None),
            P(("batch", "shard"), "seq", None),
            P(("batch", "shard"), "seq"),
            P(("batch", "shard"), None),
            P(("batch", "shard"), None),
            P(("batch", "shard"), None),
            P(("batch", "shard"), None),
            P(("batch", "shard")),
            P(("batch", "shard"), None),
            P(("batch", "shard"), None),
            P(("batch", "shard"), None),
            P(("batch", "shard"), None),
            P(("batch", "shard")),
            P(("batch", "shard"), None),
            P(("batch", "shard"), None),
            P(("batch", "shard"), None),
            P(("batch", "shard"), None),
            P(("batch", "shard")),
        ),
        out_specs=(
            P(("batch", "shard"), "seq", None),
            P(("batch", "shard"), "seq", None),
            P(("batch", "shard"), None),
            P(("batch", "shard"), None),
            P(("batch", "shard"), None),
            P(("batch", "shard"), None),
            P(("batch", "shard")),
            P(("batch", "shard"), None),
            P(("batch", "shard"), None),
            P(("batch", "shard"), None),
            P(("batch", "shard"), None),
            P(("batch", "shard")),
            P(("batch", "shard"), None),
            P(("batch", "shard"), None),
            P(("batch", "shard"), None),
            P(("batch", "shard"), None),
            P(("batch", "shard")),
        ),
        check_vma=False,
    )
```
